32 devices in a mesh: seq: 8 (over z, core), wsh: 4 (over y, x).
Axes of the slice: x: 2, y: 2, z: 4, core: 2. Of those that a mesh axis runs over, the one named last changes fastest.
Arguments:
- inputs: bfloat16 [2, 4, 1024, 2048], P(None, 'wsh', 'seq'), may hold values from -6 to 6
- segments: int32 [2, 4, 1024], P(None, 'wsh'), may hold values from 0 to 7, never falling along the last dimension, each value on 1 to 256 neighbouring positions
- cotangent: bfloat16 [2, 4, 1024, 2048], P(None, 'wsh', 'seq'), may hold values from -6 to 6
- norm1_gain: bfloat16 [2048], P('wsh'), may hold values from 0.5 to 1.5
- gate_branch_w: bfloat16 [2048, 2560], P('wsh'), may hold values from -0.125 to 0.125
- linear_branch_w: bfloat16 [2048, 2560], P('wsh'), may hold values from -0.125 to 0.125
- conv_weight: bfloat16 [2560, 4], P(('seq', 'wsh')), may hold values from -3 to 3
- input_gate_w: bfloat16 [2560, 160], P(('seq', 'wsh')), may hold values from -0.5 to 0.5
- recur_gate_w: bfloat16 [2560, 160], P(('seq', 'wsh')), may hold values from -0.5 to 0.5
- decay_param: bfloat16 [2560], P(('seq', 'wsh')), may hold values from 5 to 11
- out_proj_w: bfloat16 [2560, 2048], P('wsh'), may hold values from -0.5 to 0.5
- norm2_gain: bfloat16 [2048], P('wsh'), may hold values from 0.5 to 1.5
- mlp_gate_w: bfloat16 [2048, 6144], P('wsh'), may hold values from -0.125 to 0.125
- mlp_up_w: bfloat16 [2048, 6144], P('wsh'), may hold values from -0.125 to 0.125
- mlp_down_w: bfloat16 [6144, 2048], P('wsh'), may hold values from -0.15625 to 0.15625
Outputs:
- block_output: float32 [2, 4, 1024, 2048], P(None, 'wsh', 'seq')
- input_grad: float32 [2, 4, 1024, 2048], P(None, 'wsh', 'seq')
- norm1_gain_grad: float32 [2048], P(('seq', 'wsh'))
- gate_branch_grad: float32 [2048, 2560], P(('seq', 'wsh'))
- linear_branch_grad: float32 [2048, 2560], P(('seq', 'wsh'))
- conv_weight_grad: float32 [2560, 4], P(('seq', 'wsh'))
- input_gate_grad: float32 [2560, 160], P(('seq', 'wsh'))
- recur_gate_grad: float32 [2560, 160], P(('seq', 'wsh'))
- decay_grad: float32 [2560], P(('seq', 'wsh'))
- out_proj_grad: float32 [2560, 2048], P(('seq', 'wsh'))
- norm2_gain_grad: float32 [2048], P(('seq', 'wsh'))
- mlp_gate_grad: float32 [2048, 6144], P(('seq', 'wsh'))
- mlp_up_grad: float32 [2048, 6144], P(('seq', 'wsh'))
- mlp_down_grad: float32 [6144, 2048], P(('seq', 'wsh'))
The draws below stay inside these ranges and needn't reach their ends.
Inputs may be any that keep to these rules, and one draw needn't show every extreme that they name: `segments`: along each sequence the numbers never fall; every segment holds 1 to 256 positions, and one holds exactly that many.
All inputs are finite; a program needn't handle non-finite values.
Results may differ from the reference program's by a relative error of at most 0.017.
Values may be sent and summed in bfloat16 or wider, within the bound.
No kernel may reach another device: no remote copies, remote signals or barrier semaphores. Data moves between devices by JAX's collectives and lax.ppermute only.
A program may use at most 384 MiB of HBM per device.

```python
import math
import jax
import jax.numpy as jnp
import numpy as np
from jax import lax

D = 2048
R = 2560
FF = 6144
CONV = 4
MB = 2
SEGS = 8
BW = 160
LEN = 1024
BATCH = 4


def block_scale(stream_key, extent, pieces, smallest, largest):
    level, own = 1.0, jax.random.fold_in(stream_key, 6)
    for position, shards_of in pieces:
        draws = jnp.exp(jax.random.uniform(jax.random.fold_in(own, position), (shards_of,), jnp.float32, smallest / len(pieces), largest / len(pieces)))
        level = level * jnp.repeat(draws, extent[position] // shards_of).reshape([-1 if axis == position else 1 for axis in range(len(extent))])
    return level


def length_profile(number_of, total, reach, lean):
    weights = [(1 << 20) // math.isqrt(grade ** lean) + 1 for grade in range(2, number_of + 1)]
    rest, counts = total - reach - (number_of - 1), [1] * (number_of - 1)
    while rest > 0:
        free = [i for i in range(number_of - 1) if counts[i] < reach]
        whole, remaining = sum([weights[i] for i in free]), rest
        for i in free:
            more = min(reach - counts[i], max(1, remaining * weights[i] // whole), rest)
            counts[i] = counts[i] + more
            rest = rest - more
    return np.array([reach] + counts)


def ragged(own_key, count, total, most, slope):
    if count == 2:
        one = jax.random.randint(own_key, (), max(1, total - most), min(most, total - 1) + 1)
        return jnp.stack([one, total - one])
    lengths = jnp.asarray(length_profile(count, total, most, slope), jnp.int32)
    pairs = (count - 1) // 2
    source_of, receiver = lengths[1:1 + 2 * pairs:2], lengths[2:2 + 2 * pairs:2]
    margin = jnp.minimum(source_of - 1, most - receiver)
    shifted = jax.random.randint(jax.random.fold_in(own_key, 1), (pairs,), 0, 1 << 20) % (margin + 1)
    lengths = lengths.at[1:1 + 2 * pairs:2].set(source_of - shifted).at[2:2 + 2 * pairs:2].set(receiver + shifted)
    return lengths[jax.random.permutation(jax.random.fold_in(own_key, 2), count)]


def noise(stream_key, dims, spread, limit, pieces=(), kind=jnp.bfloat16):
    level = block_scale(stream_key, dims, pieces, -0.22, 0.18) if pieces else 1.0
    entries = jax.random.normal(stream_key, dims, jnp.float32) * spread * level
    return jnp.minimum(jnp.maximum(entries, -limit), limit).astype(kind)


def setup_inputs(seed: int = 0) -> dict:
    seeds = jax.random.split(jax.random.key(seed), 16)
    return {
        "inputs": noise(seeds[0], (MB, BATCH, LEN, D), 1.0, 6.0, ((1, 4), (2, 8))),
        "segments": jax.vmap(lambda own: jnp.searchsorted(jnp.cumsum(ragged(own, SEGS, LEN, LEN // 4, 2)), jnp.arange(LEN), side="right"))(jax.random.split(seeds[1], MB * BATCH)).reshape((MB, BATCH, LEN)).astype(jnp.int32),
        "cotangent": noise(seeds[2], (MB, BATCH, LEN, D), 1.0, 6.0, ((1, 4), (2, 8))),
        "norm1_gain": jnp.clip(1.0 + 0.1 * jax.random.normal(seeds[3], (D,), jnp.float32), 0.5, 1.5).astype(jnp.bfloat16),
        "gate_branch_w": noise(seeds[4], (D, R), D ** -0.5, 0.125, ((0, 4),)),
        "linear_branch_w": noise(seeds[5], (D, R), D ** -0.5, 0.125, ((0, 4),)),
        "conv_weight": noise(seeds[6], (R, CONV), CONV ** -0.5, 3.0, ((0, 32),)),
        "input_gate_w": noise(seeds[7], (R, BW), BW ** -0.5, 0.5, ((0, 32),)),
        "recur_gate_w": noise(seeds[8], (R, BW), BW ** -0.5, 0.5, ((0, 32),)),
        "decay_param": jnp.clip(5.0 + 6.0 * jax.random.uniform(seeds[9], (R,), jnp.float32) ** block_scale(seeds[9], (R,), ((0, 32),), -0.2, 0.2), 5.0, 11.0).astype(jnp.bfloat16),
        "out_proj_w": noise(seeds[10], (R, D), BW ** -0.5, 0.5, ((0, 4),)),
        "norm2_gain": jnp.clip(1.0 + 0.1 * jax.random.normal(seeds[11], (D,), jnp.float32), 0.5, 1.5).astype(jnp.bfloat16),
        "mlp_gate_w": noise(seeds[12], (D, FF), D ** -0.5, 0.125, ((0, 4),)),
        "mlp_up_w": noise(seeds[13], (D, FF), D ** -0.5, 0.125, ((0, 4),)),
        "mlp_down_w": noise(seeds[14], (FF, D), (FF // 4) ** -0.5, 0.15625, ((0, 4),)),
    }


EPS = 1e-06
HIGH = lax.Precision.HIGHEST

@jax.custom_vjp
def low(v):
    return lax.optimization_barrier(v.astype(jnp.bfloat16)).astype(jnp.float32)

@jax.custom_vjp
def low_back(v):
    return v

def low_keep(v):
    return (low(v), None)

def low_pass(kept, grad):
    return (grad,)

def back_keep(v):
    return (v, None)

def back_low(kept, grad):
    return (low(grad),)
low.defvjp(low_keep, low_pass)
low_back.defvjp(back_keep, back_low)

def matmul(left, right):
    return jnp.dot(left, right, precision=HIGH)

def rms_norm(values, gain):
    scale = lax.rsqrt(lax.optimization_barrier(jnp.mean(values * values, axis=-1, keepdims=True)) + EPS)
    return values * scale * gain

def reset_flags(segment_row):
    prior = jnp.concatenate([segment_row[:1] - 1, segment_row[:-1]])
    return (segment_row != prior)[:, None]

def conv_taps(values, weight, segment_row):
    total = values * weight[:, 0]
    for tap in range(1, weight.shape[1]):
        moved = jnp.concatenate([jnp.zeros((tap, values.shape[1]), values.dtype), values[:-tap]], axis=0)
        earlier = jnp.concatenate([jnp.full((tap,), -1, jnp.int32), segment_row[:-tap].astype(jnp.int32)])
        keep = (earlier == segment_row.astype(jnp.int32))[:, None]
        total = total + jnp.where(keep, moved, 0.0) * weight[:, tap]
    return total

def lru_inputs(conv_out, in_gate, rec_gate, decay, reset):
    length, width = conv_out.shape
    block = in_gate.shape[1]
    grouped = conv_out.reshape(length, width // block, block)
    gate_in = jax.nn.sigmoid(jnp.einsum('thi,hij->thj', grouped, in_gate.reshape(width // block, block, block), precision=HIGH).reshape(length, width))
    gate_rec = jax.nn.sigmoid(jnp.einsum('thi,hij->thj', grouped, rec_gate.reshape(width // block, block, block), precision=HIGH).reshape(length, width))
    log_decay = -8.0 * gate_rec * jax.nn.softplus(-decay)
    scale = jnp.where(reset, 1.0, jnp.sqrt(-jnp.expm1(2.0 * log_decay)))
    return (log_decay, scale * gate_in * conv_out)

def recurrence(log_decay, driven, reset):

    def advance(state, items):
        decay_row, drive_row, reset_row = items
        state = jnp.where(reset_row, 0.0, jnp.exp(decay_row)) * state + drive_row
        return (state, state)
    start = jnp.zeros((log_decay.shape[1],), log_decay.dtype)
    _, states = lax.scan(advance, start, (log_decay, driven, reset))
    return states

def block_forward(rows, params, segment_row):
    gain_one, w_gate, w_linear, conv_w, in_gate, rec_gate, decay, w_out, gain_two, mlp_gate, mlp_up, mlp_down = params
    normed = low(rms_norm(rows, gain_one))
    gate_pre = low_back(matmul(normed, w_gate))
    linear_pre = low(low_back(matmul(normed, w_linear)))
    gate = jax.nn.gelu(gate_pre)
    reset = reset_flags(segment_row)
    conv_out = conv_taps(linear_pre, conv_w, segment_row)
    log_decay, driven = lru_inputs(conv_out, in_gate, rec_gate, decay, reset)
    mixed = low(low_back(recurrence(log_decay, driven, reset)))
    product = low(gate * mixed)
    hidden = rows + low_back(matmul(product, w_out))
    normed_two = low(rms_norm(hidden, gain_two))
    up_gate = low_back(matmul(normed_two, mlp_gate))
    up_lin = low_back(matmul(normed_two, mlp_up))
    active = low(jax.nn.gelu(up_gate) * up_lin)
    return hidden + low_back(matmul(active, mlp_down))

def reference(inputs, segments, cotangent, norm1_gain, gate_branch_w, linear_branch_w, conv_weight, input_gate_w, recur_gate_w, decay_param, out_proj_w, norm2_gain, mlp_gate_w, mlp_up_w, mlp_down_w):
    params = tuple((item.astype(jnp.float32) for item in (norm1_gain, gate_branch_w, linear_branch_w, conv_weight, input_gate_w, recur_gate_w, decay_param, out_proj_w, norm2_gain, mlp_gate_w, mlp_up_w, mlp_down_w)))
    rows_all = inputs.astype(jnp.float32).reshape(-1, LEN, D)
    grads_all = cotangent.astype(jnp.float32).reshape(-1, LEN, D)
    segs_all = segments.reshape(-1, LEN).astype(jnp.int32)
    zeros = tuple((jnp.zeros_like(item) for item in params))

    def one_sequence(carry, items):
        rows, grad_rows, segment_row = items

        def forward(values, weights):
            return block_forward(values, weights, segment_row)
        result, backward = jax.vjp(forward, rows, params)
        grad_input, grad_params = backward(grad_rows)
        return (tuple((left + right for left, right in zip(carry, grad_params))), (result, grad_input))
    totals, (results, grad_inputs) = lax.scan(one_sequence, zeros, (rows_all, grads_all, segs_all))
    shape = inputs.shape
    return (results.reshape(shape), grad_inputs.reshape(shape), totals[0], totals[1], totals[2], totals[3], totals[4], totals[5], totals[6], totals[7], totals[8], totals[9], totals[10], totals[11])
```

```python
from functools import partial

import jax
import jax.numpy as jnp
from jax import lax
from jax.experimental import pallas as pl
from jax.experimental.pallas import tpu as pltpu
from jax.sharding import PartitionSpec as P

EPS = 1e-06
AXES = ("seq", "wsh")
LANES = 128
VMEM_LIMIT = 48 * 1024 * 1024
f32 = jnp.float32
bf16 = jnp.bfloat16


def gelu_parts(v):
    k = 0.7978845608028654
    t = jnp.tanh(k * (v + 0.044715 * v * v * v))
    half = 0.5 * (1.0 + t)
    slope = half + 0.5 * v * (1.0 - t * t) * k * (1.0 + 3.0 * 0.044715 * v * v)
    return v * half, slope


def lru_parts(zr, soft):
    rg = jax.nn.sigmoid(zr)
    la = -8.0 * rg * soft
    a = jnp.exp(la)
    x = 2.0 * la
    series = -x * (
        1.0
        + x
        * (
            1.0 / 2.0
            + x
            * (
                1.0 / 6.0
                + x
                * (
                    1.0 / 24.0
                    + x * (1.0 / 120.0 + x * (1.0 / 720.0 + x * (1.0 / 5040.0 + x * (1.0 / 40320.0))))
                )
            )
        )
    )
    rest = jnp.where(x > -0.5, series, 1.0 - a * a)
    return rg, a, rest


def conv_kernel(T, Q, taps, pre_ref, halo_ref, mask_ref, w_ref, conv_ref):
    w = [w_ref[k : k + 1, :] for k in range(taps)]
    past = tuple(halo_ref[pl.ds((taps - 2 - k) * Q, Q), :] for k in range(taps - 1))

    def step(t, past):
        u = pre_ref[pl.ds(t, Q, stride=T), :].astype(bf16).astype(f32)
        row = pl.multiple_of(t * Q, Q)
        depth = mask_ref[pl.ds(row, Q), :]
        total = w[0] * u
        for k in range(1, taps):
            total = total + jnp.where(depth >= k, past[k - 1], 0.0) * w[k]
        conv_ref[pl.ds(row, Q), :] = total
        return (u,) + past[:-1]

    lax.fori_loop(0, T, step, past, unroll=8)


def scan_kernel(T, Q, zi_ref, zr_ref, conv_ref, mask_ref, soft_ref, h_ref, a_ref, end_ref):
    soft = soft_ref[0:1, :]

    def step(t, carry):
        h, prod = carry
        rows = pl.ds(pl.multiple_of(t * Q, Q), Q)
        keep = mask_ref[rows, :] >= 1.0
        ig = jax.nn.sigmoid(zi_ref[rows, :])
        _, a, rest = lru_parts(zr_ref[rows, :], soft)
        mult = jnp.where(keep, jnp.sqrt(rest), 1.0)
        a = jnp.where(keep, a, 0.0)
        h = a * h + mult * ig * conv_ref[rows, :]
        prod = prod * a
        h_ref[rows, :] = h
        a_ref[rows, :] = a
        return h, prod

    zero = jnp.zeros((Q, h_ref.shape[1]), f32)
    h, prod = lax.fori_loop(0, T, step, (zero, zero + 1.0), unroll=8)
    end_ref[0:Q, :] = h
    end_ref[Q : 2 * Q, :] = prod


def carry_kernel(T, Q, h_ref, a_ref, carry_ref, ypre_ref, state_ref, hs_ref, prod_ref, tmp_ref):
    def step(t, carried):
        rows = pl.ds(pl.multiple_of(t * Q, Q), Q)
        carried = carried * a_ref[rows, :]
        h = h_ref[rows, :] + carried
        state_ref[rows, :] = h
        tmp_ref[pl.ds(t, Q, stride=T), :] = h
        return carried

    lax.fori_loop(0, T, step, carry_ref[...], unroll=8)

    def block(i, _):
        rows = pl.ds(pl.multiple_of(i * 64, 64), 64)
        hs = tmp_ref[rows, :].astype(bf16)
        hs_ref[rows, :] = hs
        gate, _ = gelu_parts(ypre_ref[rows, :])
        prod_ref[rows, :] = (gate * hs.astype(f32)).astype(bf16)
        return 0

    lax.fori_loop(0, T * Q // 64, block, 0)


def back_scan_kernel(T, Q, dprod_ref, ypre_ref, hs_ref, a_ref, dy_ref, e_ref, first_ref, tmp_ref):
    def block(i, _):
        rows = pl.ds(pl.multiple_of(i * 64, 64), 64)
        dprod = dprod_ref[rows, :]
        gate, slope = gelu_parts(ypre_ref[rows, :])
        dy_ref[rows, :] = (dprod * hs_ref[rows, :].astype(f32) * slope).astype(bf16)
        tmp_ref[rows, :] = (dprod * gate).astype(bf16).astype(f32)
        return 0

    lax.fori_loop(0, T * Q // 64, block, 0)

    def step(i, moved):
        t = T - 1 - i
        rows = pl.ds(pl.multiple_of(t * Q, Q), Q)
        e = tmp_ref[pl.ds(t, Q, stride=T), :] + moved
        e_ref[rows, :] = e
        return e * a_ref[rows, :]

    zero = jnp.zeros((Q, e_ref.shape[1]), f32)
    first_ref[...] = lax.fori_loop(0, T, step, zero, unroll=8)


def back_gates_kernel(
    T,
    Q,
    e_ref,
    right_ref,
    zi_ref,
    zr_ref,
    conv_ref,
    state_ref,
    carry_ref,
    mask_ref,
    soft_ref,
    dzi_ref,
    dzr_ref,
    dconv_ref,
    ddecay_ref,
    tmpi_ref,
    tmpr_ref,
):
    soft = soft_ref[0:1, :]
    sig = soft_ref[1:2, :]

    def one(t, moved, total, prior):
        rows = pl.ds(pl.multiple_of(t * Q, Q), Q)
        keep = mask_ref[rows, :] >= 1.0
        e = e_ref[rows, :] + moved
        ig = jax.nn.sigmoid(zi_ref[rows, :])
        rg, a, rest = lru_parts(zr_ref[rows, :], soft)
        conv = conv_ref[rows, :]
        mult = jnp.where(keep, jnp.sqrt(rest), 1.0)
        dla = jnp.where(keep, e * a * prior - e * ig * conv * (a * a) / mult, 0.0)
        total = total + dla * rg
        tmpr_ref[rows, :] = dla * (-8.0 * soft) * rg * (1.0 - rg)
        em = e * mult
        tmpi_ref[rows, :] = em * conv * ig * (1.0 - ig)
        dconv_ref[rows, :] = em * ig
        return moved * jnp.where(keep, a, 0.0), total

    def step(i, carry):
        moved, total = carry
        t = T - 1 - i
        prior = state_ref[pl.ds(pl.multiple_of((t - 1) * Q, Q), Q), :]
        return one(t, moved, total, prior)

    zero = jnp.zeros((Q, e_ref.shape[1]), f32)
    moved, total = lax.fori_loop(0, T - 1, step, (right_ref[...], zero), unroll=4)
    _, total = one(0, moved, total, carry_ref[...])
    ddecay_ref[...] = 8.0 * sig * jnp.sum(total, axis=0, keepdims=True)

    def block(i, _):
        rows = pl.ds(pl.multiple_of(i * 64, 64), 64)
        dzi_ref[rows, :] = tmpi_ref[rows, :].astype(bf16)
        dzr_ref[rows, :] = tmpr_ref[rows, :].astype(bf16)
        return 0

    lax.fori_loop(0, T * Q // 64, block, 0)


def back_conv_kernel(
    T, Q, taps, dconv_ref, next_ref, pre_ref, halo_ref, mask_ref, w_ref, dus_ref, dw_ref, tmp_ref
):
    w = [w_ref[k : k + 1, :] for k in range(taps)]
    past = tuple(halo_ref[pl.ds((taps - 2 - k) * Q, Q), :] for k in range(taps - 1))
    zero = jnp.zeros((Q, pre_ref.shape[1]), f32)

    def terms(dconv, depth):
        return tuple(jnp.where(depth >= k, dconv, 0.0) for k in range(1, taps))

    def step(t, carry):
        past, waiting, sums = carry
        u = pre_ref[pl.ds(t, Q, stride=T), :].astype(bf16).astype(f32)
        rows = pl.ds(pl.multiple_of(t * Q, Q), Q)
        dconv = dconv_ref[rows, :]
        masked = terms(dconv, mask_ref[rows, :])
        done = waiting[taps - 2] + w[taps - 1] * masked[taps - 2]
        older = [w[0] * dconv]
        for k in range(1, taps - 1):
            older.append(waiting[k - 1] + w[k] * masked[k - 1])
        sums = (sums[0] + dconv * u,) + tuple(
            sums[k] + masked[k - 1] * past[k - 1] for k in range(1, taps)
        )

        @pl.when(t >= taps - 1)
        def _():
            tmp_ref[pl.ds(t - (taps - 1), Q, stride=T), :] = done

        return (u,) + past[:-1], tuple(older), sums

    start = (past, (zero,) * (taps - 1), (zero,) * taps)
    _, waiting, sums = lax.fori_loop(0, T, step, start, unroll=4)
    for j in range(taps - 1):
        rows = pl.ds(j * Q, Q)
        masked = terms(next_ref[rows, :], mask_ref[pl.ds((T + j) * Q, Q), :])
        done = waiting[taps - 2] + w[taps - 1] * masked[taps - 2]
        older = [zero]
        for k in range(1, taps - 1):
            older.append(waiting[k - 1] + w[k] * masked[k - 1])
        tmp_ref[pl.ds(T + j - (taps - 1), Q, stride=T), :] = done
        waiting = tuple(older)
    for k in range(taps):
        dw_ref[k : k + 1, :] = jnp.sum(sums[k], axis=0, keepdims=True)

    def block(i, _):
        rows = pl.ds(pl.multiple_of(i * 64, 64), 64)
        dus_ref[rows, :] = tmp_ref[rows, :].astype(bf16)
        return 0

    lax.fori_loop(0, T * Q // 64, block, 0)


def tiled_call(kernel, ins, outs, scratch=()):
    channels = outs[0][0][1]

    def spec(shape, first):
        return pl.BlockSpec((shape[0], LANES), (lambda c: (0, 0)) if first is None else (lambda c: (0, c + first)))

    moved = sum(a.size * a.dtype.itemsize for a, _ in ins)
    moved += sum(shape[0] * shape[1] * jnp.dtype(kind).itemsize for shape, kind in outs)
    work = outs[0][0][0] * channels
    return pl.pallas_call(
        kernel,
        grid=(pl.cdiv(channels, LANES),),
        in_specs=[spec(a.shape, first) for a, first in ins],
        out_specs=[spec(shape, 0) for shape, _ in outs],
        out_shape=[jax.ShapeDtypeStruct(shape, kind) for shape, kind in outs],
        scratch_shapes=[pltpu.VMEM((rows, LANES), f32) for rows in scratch],
        compiler_params=pltpu.CompilerParams(vmem_limit_bytes=VMEM_LIMIT),
        cost_estimate=pl.CostEstimate(flops=40 * work, bytes_accessed=moved, transcendentals=4 * work),
    )(*[a for a, _ in ins])


def assemble(places, blocks, rows_total, part, count, weights):
    columns = blocks[0].shape[1] // weights
    copies_total = ((len(blocks) - 1) * count + 1) * weights

    def kernel(places_ref, *refs):
        sources, outs, sems = refs[: len(blocks)], refs[len(blocks) : -1], refs[-1]
        copies = []

        def put(ref, start, rows, i):
            at = pl.multiple_of(places_ref[i], 16)
            for k, out in enumerate(outs):
                source = ref.at[pl.ds(start, rows), pl.ds(k * columns, columns)]
                copy = pltpu.make_async_copy(source, out.at[pl.ds(at, rows), :], sems.at[len(copies)])
                copy.start()
                copies.append(copy)

        i = 0
        for ref in sources[:-1]:
            for j in range(count):
                put(ref, j * part, part, i)
                i += 1
        put(sources[-1], 0, sources[-1].shape[0], i)
        for copy in copies:
            copy.wait()

    return pl.pallas_call(
        kernel,
        in_specs=[pl.BlockSpec(memory_space=pltpu.SMEM)] + [pl.BlockSpec(memory_space=pl.ANY)] * len(blocks),
        out_specs=[pl.BlockSpec(memory_space=pltpu.VMEM)] * weights,
        out_shape=[jax.ShapeDtypeStruct((rows_total, columns), blocks[0].dtype)] * weights,
        scratch_shapes=[pltpu.SemaphoreType.DMA((copies_total,))],
        compiler_params=pltpu.CompilerParams(vmem_limit_bytes=VMEM_LIMIT),
        cost_estimate=pl.CostEstimate(
            flops=0, bytes_accessed=4 * rows_total * columns * weights, transcendentals=0
        ),
    )(places, *blocks)


def norm_rows(pieces, gain, rows):
    width = pieces[0].shape[1]
    step = 16

    def kernel(gain_ref, *refs):
        out_ref = refs[-1]
        for i, ref in enumerate(refs[:-1]):

            @pl.when(pl.program_id(0) == i)
            def _():
                def body(k, _):
                    at = pl.ds(pl.multiple_of(k * step, step), step)
                    v = ref[at, :].astype(f32)
                    scale = lax.rsqrt(jnp.mean(v * v, axis=-1, keepdims=True) + EPS)
                    out_ref[at, :] = (v * scale * gain_ref[0:1, :]).astype(bf16)
                    return 0

                lax.fori_loop(0, rows // step, body, 0)

    return pl.pallas_call(
        kernel,
        grid=(len(pieces),),
        in_specs=[pl.BlockSpec((8, width), lambda i: (0, 0))]
        + [pl.BlockSpec(p.shape, lambda i: (0, 0)) for p in pieces],
        out_specs=pl.BlockSpec((rows, width), lambda i: (i, 0)),
        out_shape=jax.ShapeDtypeStruct((rows * len(pieces), width), bf16),
        compiler_params=pltpu.CompilerParams(vmem_limit_bytes=VMEM_LIMIT),
        cost_estimate=pl.CostEstimate(
            flops=6 * rows * len(pieces) * width,
            bytes_accessed=4 * rows * len(pieces) * width,
            transcendentals=0,
        ),
    )(jnp.broadcast_to(gain[None, :], (8, width)), *pieces)


def after(value, *others):
    return lax.optimization_barrier((value,) + others)[0]


def per_device(
    seqs,
    wide,
    inputs,
    segments,
    cotangent,
    norm1_gain,
    gate_branch_w,
    linear_branch_w,
    conv_weight,
    input_gate_w,
    recur_gate_w,
    decay_param,
    out_proj_w,
    norm2_gain,
    mlp_gate_w,
    mlp_up_w,
    mlp_down_w,
):
    micro, _, T, D = inputs.shape
    length = segments.shape[2]
    Q = micro * wide
    chips = seqs // 2
    C = gate_branch_w.shape[1] // wide
    tiles = pl.cdiv(C, LANES)
    wide_C = tiles * LANES
    F = mlp_gate_w.shape[1] // wide
    block = input_gate_w.shape[1]
    taps = conv_weight.shape[1]
    own = micro * T
    shard = D // wide
    seq = lax.axis_index("seq")
    wsh = lax.axis_index("wsh")
    chip, core = seq // 2, seq % 2

    def perm_of(move_seq, flip=0):
        pairs = [(s, move_seq(s), w) for s in range(seqs) for w in range(wide)]
        return [(s * wide + w, d * wide + (w ^ flip)) for s, d, w in pairs if 0 <= d < seqs]

    def along_wsh(flip):
        return perm_of(lambda s: s, flip)

    def along_seq(shift):
        return perm_of(lambda s: s + shift)

    twin_perm = perm_of(lambda s: s ^ 1)
    pair_perm = perm_of(lambda s: s ^ 2)
    ring_perm = perm_of(lambda s: (s + 2) % seqs)
    from_owner = [(k // wide * wide + k % wide, k % seqs * wide + k // seqs) for k in range(seqs * wide)]
    halves_to_owner = []
    for w in range(wide):
        for s in range(seqs):
            halves_to_owner.append((s * wide + w, w * seqs + s % 2 * chips + s // 2))

    def send(value, perm):
        return lax.ppermute(value, AXES, perm)

    def spread(piece):
        return [piece] + [send(piece, along_wsh(r)) for r in range(1, wide)]

    def collect(products):
        got = [send(products[r].astype(bf16), along_wsh(r)) for r in range(wide - 1, 0, -1)]
        total = products[0]
        for value in got:
            total = total + value.astype(f32)
        return total

    def token_rows(value, r):
        return value[r * own : (r + 1) * own]

    def own_columns(weights, r, start, rows):
        parts = []
        for weight in weights:
            columns = weight.shape[1] // wide
            value = lax.dynamic_slice(weight, (start, (wsh ^ r) * columns), (rows, columns))
            parts.append(jnp.pad(value, ((0, 0), (0, -columns % LANES))))
        return jnp.concatenate(parts, axis=1)

    def fetch(weights, rows, at):
        got = [send(own_columns(weights, r, at * rows, rows), along_wsh(r)) for r in range(wide - 1, 0, -1)]
        return jnp.concatenate(got[::-1], axis=0)

    def place(weights, fetched, rows):
        places = [(wsh ^ r) * shard + at * rows for _, at in fetched for r in range(1, wide)]
        places = jnp.stack(places + [wsh * shard]).astype(jnp.int32)
        blocks = [value for value, _ in fetched] + [own_columns(weights, 0, 0, shard)]
        out = assemble(places, blocks, D, rows, wide - 1, len(weights))
        return [value[:, : w.shape[1] // wide] for value, w in zip(out, weights)]

    def pair_sums(terms):
        pairs = []
        for k in list(range(1, chips)) + [0]:
            target = lax.rem(chip - k + chips, chips)
            other = send(terms(target, 1 - core).astype(bf16), twin_perm)
            pairs.append((terms(target, core) + other.astype(f32)).astype(bf16))
        return list(lax.optimization_barrier(tuple(pairs)))

    def ring_step(held, pair):
        return send(held.astype(bf16), ring_perm).astype(f32) + pair.astype(f32)

    def ring_sum(pairs):
        held = pairs[0]
        for pair in pairs[1:]:
            held = ring_step(held, pair)
        return held

    def strided_terms(left, right):
        n = left.shape[1] // seqs

        def terms(target, half):
            return t_dot(lax.dynamic_slice(left, (0, (2 * target + half) * n), (left.shape[0], n)), right)

        return terms

    def halved_terms(left, right):
        n = left.shape[1] // seqs

        def terms(target, half):
            return t_dot(lax.dynamic_slice(left, (0, (half * chips + target) * n), (left.shape[0], n)), right)

        return terms

    def columns_to_rows(value, weights, gain):
        rows = value.shape[0]
        weight_rows = [lax.dynamic_slice(w, (seq * rows, 0), (rows, w.shape[1])) for w in weights]
        weight_rows = jnp.concatenate(weight_rows, axis=1).astype(f32)
        own_gain = lax.dynamic_slice(gain, (seq * rows,), (rows,))
        term = jnp.sum(value * weight_rows, axis=1) / own_gain
        low = value.astype(bf16).reshape(rows, 2, -1)
        term_low = term.astype(bf16)
        rest = (term - term_low.astype(f32)).astype(bf16)
        extra = jnp.pad(jnp.stack([term_low, rest], axis=1)[:, :, None], ((0, 0), (0, 0), (0, LANES - 1)))
        n = low.shape[2]
        low = jnp.concatenate([low, extra], axis=2)
        got = lax.all_to_all(low, "wsh", split_axis=0, concat_axis=2, tiled=True).astype(f32)
        got = got.reshape(rows // wide, 2, wide, n + LANES)
        grads = got[:, :, :, :n].reshape(rows // wide, 2, wide * n)
        return grads[:, 0], grads[:, 1], jnp.sum(got[:, :, :, n], axis=(1, 2))

    def dot(a, b):
        return jnp.dot(a, b, preferred_element_type=f32)

    def dot_t(a, b):
        return lax.dot_general(a, b, (((1,), (1,)), ((), ())), preferred_element_type=f32)

    def t_dot(a, b):
        return lax.dot_general(a, b, (((0,), (0,)), ((), ())), preferred_element_type=f32)

    def scale_of(v):
        return lax.rsqrt(jnp.mean(v * v, axis=-1, keepdims=True) + EPS)

    def norm_back(dn, v, gain):
        s = scale_of(v)
        scaled = dn * gain
        return s * scaled - v * (s * s * s) * jnp.mean(scaled * v, axis=-1, keepdims=True)

    branch = [gate_branch_w, linear_branch_w]
    branch_rows = shard // 4
    held = fetch(branch, branch_rows, seq % 4)
    paired = send(held, pair_perm)
    here, there = seq % 4, seq % 4 ^ 2
    branch_parts = [
        (held, here),
        (paired, there),
        (send(held, twin_perm), here ^ 1),
        (send(paired, twin_perm), there ^ 1),
    ]
    w_gate, w_linear = place(branch, branch_parts, branch_rows)

    rows = jnp.pad(segments[:, 0], ((0, 0), (taps - 1, taps - 1)), constant_values=-1)
    whole_depth = jnp.zeros((micro, length + taps - 1), f32)
    for k in range(1, taps):
        same = rows[:, taps - 1 :] == rows[:, taps - 1 - k : rows.shape[1] - k]
        same = same & (jnp.arange(length + taps - 1) >= k)[None, :]
        whole_depth = whole_depth + same.astype(f32)
    depth = lax.dynamic_slice(whole_depth, (0, seq * T), (micro, T + taps - 1)).astype(bf16)

    note = jnp.zeros((16, D), bf16)
    note = note.at[:micro, : T + taps - 1].set(depth)
    note = note.at[micro, :shard].set(norm1_gain)
    note = note.at[micro + 1, :shard].set(norm2_gain)
    noted = jnp.concatenate([inputs[:, 0].reshape(own, D), note], axis=0)
    x_pieces = spread(after(noted, held))
    notes = [piece[own:] for piece in x_pieces]
    depth = jnp.concatenate([n[:micro, : T + taps - 1] for n in notes], axis=0).astype(f32)
    mask = jnp.broadcast_to(depth.T[:, :, None], (T + taps - 1, Q, LANES)).reshape(-1, LANES)
    mask_own = mask[: T * Q]

    def joined(k):
        whole = jnp.zeros((D,), bf16)
        for r in range(wide):
            whole = lax.dynamic_update_slice(whole, notes[r][micro + k, :shard], ((wsh ^ r) * shard,))
        return whole.astype(f32)

    gain_one, gain_two = joined(0), joined(1)
    small = jnp.concatenate([input_gate_w, recur_gate_w, conv_weight, decay_param[:, None]], axis=1)
    pad = -small.shape[1] % LANES
    small = send(jnp.pad(small, ((0, 0), (0, pad))), from_owner)
    small = lax.all_gather(small, "seq", axis=0, tiled=True)
    in_gate = small[:, :block]
    rec_gate = small[:, block : 2 * block]
    conv_w = small[:, 2 * block : 2 * block + taps].astype(f32).T
    conv_w = jnp.pad(conv_w, ((0, 8 - taps), (0, 0)))
    decay = small[:, 2 * block + taps].astype(f32)
    soft = jnp.stack([jax.nn.softplus(-decay), jax.nn.sigmoid(-decay)])
    soft = jnp.pad(soft, ((0, 6), (0, 0)))
    blocks = C // block
    eye = jnp.eye(blocks, dtype=bf16)

    def dense(gate_w):
        spread_w = gate_w.reshape(blocks, block, 1, block) * eye[:, None, :, None]
        return jnp.pad(spread_w.reshape(C, C), ((0, 0), (0, wide_C - C)))

    gates_w = jnp.concatenate([dense(in_gate), dense(rec_gate)], axis=1)

    xn = norm_rows(x_pieces, gain_one, own)
    last = xn.reshape(Q, T, D)[:, T - (taps - 1) :].transpose(1, 0, 2).reshape((taps - 1) * Q, D)
    halo = send(dot(last, w_linear).astype(bf16), along_seq(1)).astype(f32)
    us_pre = dot(xn, w_linear)

    mlp = [mlp_gate_w, mlp_up_w]
    mlp_rows = shard // seqs
    held = fetch([after(w, *x_pieces[1:]) for w in mlp], mlp_rows, seq)
    mlp_parts = []
    for k in range(chips):
        if k:
            held = send(held, ring_perm)
        source = lax.rem(chip - k + chips, chips) * 2
        mlp_parts.append((held, source + core))
        mlp_parts.append((send(held, twin_perm), source + 1 - core))

    (conv,) = tiled_call(
        partial(conv_kernel, T, Q, taps),
        [(us_pre, 0), (halo, 0), (mask_own, None), (conv_w, 0)],
        [((T * Q, C), f32)],
    )
    conv_low = conv.astype(bf16)
    z = dot(conv_low, gates_w)
    h_local, a, end = tiled_call(
        partial(scan_kernel, T, Q),
        [(z, 0), (z, tiles), (conv, 0), (mask_own, None), (soft, 0)],
        [((T * Q, C), f32), ((T * Q, C), f32), ((2 * Q, C), f32)],
    )
    reach = pl.cdiv(length // 4, T)
    ends = [send(end, along_seq(k)) for k in range(1, reach + 1)]
    ypre = dot(after(xn, end), w_gate)
    carry, through = ends[0][:Q], ends[0][Q:]
    for value in ends[1:]:
        carry = carry + through * value[:Q]
        through = through * value[Q:]
    state, hs, prod = tiled_call(
        partial(carry_kernel, T, Q),
        [(h_local, 0), (a, 0), (carry, 0), (ypre, 0)],
        [((T * Q, C), f32), ((T * Q, C), bf16), ((T * Q, C), bf16)],
        [T * Q],
    )
    following_ends = [send(end[Q:], along_seq(-k)) for k in range(1, reach)]

    x_own = inputs[:, 0].reshape(own, D).astype(f32)
    hidden = x_own + collect([dot(token_rows(prod, r), out_proj_w) for r in range(wide)])
    hn_own = (hidden * scale_of(hidden) * gain_two).astype(bf16)
    hn_pieces = spread(hn_own)
    hn = jnp.concatenate(hn_pieces, axis=0)
    w_gate2, w_up = place(mlp, mlp_parts, mlp_rows)
    g_pieces = spread(after(cotangent[:, 0].reshape(own, D), *hn_pieces[1:]))
    gpre = dot(hn, w_gate2)
    uppre = dot(hn, w_up)
    act_gate, act_slope = gelu_parts(gpre)
    act = (act_gate * uppre).astype(bf16)

    g_group = jnp.concatenate(g_pieces, axis=0)
    g_own = cotangent[:, 0].reshape(own, D).astype(f32)
    dact = dot_t(g_group, mlp_down_w)
    dgp = (dact * uppre * act_slope).astype(bf16)
    dup = (dact * act_gate).astype(bf16)
    products = [dot_t(token_rows(dgp, r), w_gate2) + dot_t(token_rows(dup, r), w_up) for r in range(wide)]
    products = [products[0]] + [p.astype(bf16) for p in products[1:]]
    dhn = collect(products)
    down_pairs = pair_sums(halved_terms(after(act, *products[1:]), g_group))
    mlp_pairs = pair_sums(strided_terms(after(hn, *products[1:]), jnp.concatenate([dgp, dup], axis=1)))
    down_sum = ring_sum(down_pairs)
    mlp_sum = ring_sum([after(mlp_pairs[0], down_sum)] + mlp_pairs[1:])
    dh1 = g_own + norm_back(dhn, hidden, gain_two)

    do_own = dh1.astype(bf16)
    do_pieces = spread(do_own)
    do = jnp.concatenate(do_pieces, axis=0)
    act_late = after(act, *do_pieces[1:])
    block_output = hidden + collect([dot(token_rows(act_late, r), mlp_down_w) for r in range(wide)])
    dprod = dot_t(do, out_proj_w)
    dy, e_local, first = tiled_call(
        partial(back_scan_kernel, T, Q),
        [(dprod, 0), (ypre, 0), (hs, 0), (a, 0)],
        [((T * Q, C), bf16), ((T * Q, C), f32), ((Q, C), f32)],
        [T * Q],
    )
    firsts = [send(first, along_seq(-k)) for k in range(1, reach + 1)]
    out_pairs = pair_sums(halved_terms(after(prod, first), do))
    right, through = firsts[0], None
    for value, past in zip(firsts[1:], following_ends):
        through = past if through is None else through * past
        right = right + through * value
    dzi, dzr, dconv_direct, ddecay = tiled_call(
        partial(back_gates_kernel, T, Q),
        [
            (e_local, 0),
            (right, 0),
            (z, 0),
            (z, tiles),
            (conv, 0),
            (state, 0),
            (carry, 0),
            (mask_own, None),
            (soft, 0),
        ],
        [((T * Q, C), bf16), ((T * Q, C), bf16), ((T * Q, C), f32), ((1, C), f32)],
        [T * Q, T * Q],
    )
    dconv = dconv_direct + dot_t(dzi, gates_w[:, :C]) + dot_t(dzr, gates_w[:, wide_C : wide_C + C])
    following = send(dconv[: (taps - 1) * Q].astype(bf16), along_seq(-1)).astype(f32)
    dus, dconv_w = tiled_call(
        partial(back_conv_kernel, T, Q, taps),
        [(dconv, 0), (following, 0), (us_pre, 0), (halo, 0), (mask, None), (conv_w, 0)],
        [((T * Q, C), bf16), ((8, C), f32)],
        [T * Q],
    )

    products = [dot_t(token_rows(dy, r), w_gate) + dot_t(token_rows(dus, r), w_linear) for r in range(wide)]
    products = [products[0]] + [p.astype(bf16) for p in products[1:]]
    dxn = collect(products)
    branch_pairs = pair_sums(strided_terms(after(xn, *products[1:]), jnp.concatenate([dy, dus], axis=1)))
    out_sum = ring_sum([after(out_pairs[0], mlp_sum)] + out_pairs[1:])
    branch_sum = ring_sum(branch_pairs)

    def diagonal(terms):
        return jnp.concatenate(
            [terms[b * block : (b + 1) * block, b * block : (b + 1) * block] for b in range(blocks)], axis=0
        )

    late_low = after(conv_low, *products[1:])
    small_terms = jnp.concatenate(
        [
            diagonal(t_dot(late_low, dzi)),
            diagonal(t_dot(late_low, dzr)),
            dconv_w[:taps].T,
            ddecay.T,
            jnp.zeros((C, pad), f32),
        ],
        axis=1,
    )

    def small_chunk(target, half):
        n = C // seqs
        return lax.dynamic_slice(small_terms, ((half * chips + target) * n, 0), (n, small_terms.shape[1]))

    small_sum = ring_sum(pair_sums(small_chunk))
    input_grad = dh1 + norm_back(dxn, x_own, gain_one)

    def owned(value):
        return send(value.astype(bf16), halves_to_owner).astype(f32)

    small_grad = owned(small_sum)
    gate2_grad, up_grad, gain_two_grad = columns_to_rows(mlp_sum, [w_gate2, w_up], gain_two)
    gate_grad, linear_grad, gain_one_grad = columns_to_rows(branch_sum, [w_gate, w_linear], gain_one)
    return (
        block_output.reshape(inputs.shape),
        input_grad.reshape(inputs.shape),
        gain_one_grad,
        gate_grad,
        linear_grad,
        small_grad[:, 2 * block : 2 * block + taps],
        small_grad[:, :block],
        small_grad[:, block : 2 * block],
        small_grad[:, 2 * block + taps],
        owned(out_sum),
        gain_two_grad,
        gate2_grad,
        up_grad,
        owned(down_sum),
    )


def solution(mesh):
    both = ("seq", "wsh")
    tokens = P(None, "wsh", "seq", None)
    return jax.shard_map(
        partial(per_device, mesh.shape["seq"], mesh.shape["wsh"]),
        mesh=mesh,
        in_specs=(
            tokens,
            P(None, "wsh", None),
            tokens,
            P("wsh"),
            P("wsh", None),
            P("wsh", None),
            P(both, None),
            P(both, None),
            P(both, None),
            P(both),
            P("wsh", None),
            P("wsh"),
            P("wsh", None),
            P("wsh", None),
            P("wsh", None),
        ),
        out_specs=(
            tokens,
            tokens,
            P(both),
            P(both, None),
            P(both, None),
            P(both, None),
            P(both, None),
            P(both, None),
            P(both),
            P(both, None),
            P(both),
            P(both, None),
            P(both, None),
            P(both, None),
        ),
        check_vma=False,
    )
```

```python
from functools import partial

import jax
import jax.numpy as jnp
from jax import lax
from jax.experimental import pallas as pl
from jax.experimental.pallas import tpu as pltpu
from jax.sharding import PartitionSpec as P

EPS = 1e-06
AXES = ("seq", "wsh")
LANES = 128
VMEM_LIMIT = 48 * 1024 * 1024
f32 = jnp.float32
bf16 = jnp.bfloat16


def gelu_parts(v):
    k = 0.7978845608028654
    t = jnp.tanh(k * (v + 0.044715 * v * v * v))
    half = 0.5 * (1.0 + t)
    slope = half + 0.5 * v * (1.0 - t * t) * k * (1.0 + 3.0 * 0.044715 * v * v)
    return v * half, slope


def lru_parts(zr, soft):
    rg = jax.nn.sigmoid(zr)
    la = -8.0 * rg * soft
    a = jnp.exp(la)
    x = 2.0 * la
    series = -x * (
        1.0
        + x
        * (
            1.0 / 2.0
            + x
            * (
                1.0 / 6.0
                + x
                * (
                    1.0 / 24.0
                    + x * (1.0 / 120.0 + x * (1.0 / 720.0 + x * (1.0 / 5040.0 + x * (1.0 / 40320.0))))
                )
            )
        )
    )
    rest = jnp.where(x > -0.5, series, 1.0 - a * a)
    return rg, a, rest


def conv_kernel(T, Q, taps, pre_ref, halo_ref, mask_ref, w_ref, conv_ref):
    w = [w_ref[k : k + 1, :] for k in range(taps)]
    past = tuple(halo_ref[pl.ds((taps - 2 - k) * Q, Q), :] for k in range(taps - 1))

    def step(t, past):
        u = pre_ref[pl.ds(t, Q, stride=T), :].astype(bf16).astype(f32)
        row = pl.multiple_of(t * Q, Q)
        depth = mask_ref[pl.ds(row, Q), :]
        total = w[0] * u
        for k in range(1, taps):
            total = total + jnp.where(depth >= k, past[k - 1], 0.0) * w[k]
        conv_ref[pl.ds(row, Q), :] = total
        return (u,) + past[:-1]

    lax.fori_loop(0, T, step, past, unroll=8)


def scan_kernel(T, Q, zi_ref, zr_ref, conv_ref, mask_ref, soft_ref, h_ref, a_ref, end_ref):
    soft = soft_ref[0:1, :]

    def step(t, carry):
        h, prod = carry
        rows = pl.ds(pl.multiple_of(t * Q, Q), Q)
        keep = mask_ref[rows, :] >= 1.0
        ig = jax.nn.sigmoid(zi_ref[rows, :])
        _, a, rest = lru_parts(zr_ref[rows, :], soft)
        mult = jnp.where(keep, jnp.sqrt(rest), 1.0)
        a = jnp.where(keep, a, 0.0)
        h = a * h + mult * ig * conv_ref[rows, :]
        prod = prod * a
        h_ref[rows, :] = h
        a_ref[rows, :] = a
        return h, prod

    zero = jnp.zeros((Q, h_ref.shape[1]), f32)
    h, prod = lax.fori_loop(0, T, step, (zero, zero + 1.0), unroll=8)
    end_ref[0:Q, :] = h
    end_ref[Q : 2 * Q, :] = prod


def carry_kernel(T, Q, h_ref, a_ref, carry_ref, ypre_ref, state_ref, hs_ref, prod_ref, tmp_ref):
    def step(t, carried):
        rows = pl.ds(pl.multiple_of(t * Q, Q), Q)
        carried = carried * a_ref[rows, :]
        h = h_ref[rows, :] + carried
        state_ref[rows, :] = h
        tmp_ref[pl.ds(t, Q, stride=T), :] = h
        return carried

    lax.fori_loop(0, T, step, carry_ref[...], unroll=8)

    def block(i, _):
        rows = pl.ds(pl.multiple_of(i * 64, 64), 64)
        hs = tmp_ref[rows, :].astype(bf16)
        hs_ref[rows, :] = hs
        gate, _ = gelu_parts(ypre_ref[rows, :])
        prod_ref[rows, :] = (gate * hs.astype(f32)).astype(bf16)
        return 0

    lax.fori_loop(0, T * Q // 64, block, 0)


def back_scan_kernel(T, Q, dprod_ref, ypre_ref, hs_ref, a_ref, dy_ref, e_ref, first_ref, tmp_ref):
    def block(i, _):
        rows = pl.ds(pl.multiple_of(i * 64, 64), 64)
        dprod = dprod_ref[rows, :]
        gate, slope = gelu_parts(ypre_ref[rows, :])
        dy_ref[rows, :] = (dprod * hs_ref[rows, :].astype(f32) * slope).astype(bf16)
        tmp_ref[rows, :] = (dprod * gate).astype(bf16).astype(f32)
        return 0

    lax.fori_loop(0, T * Q // 64, block, 0)

    def step(i, moved):
        t = T - 1 - i
        rows = pl.ds(pl.multiple_of(t * Q, Q), Q)
        e = tmp_ref[pl.ds(t, Q, stride=T), :] + moved
        e_ref[rows, :] = e
        return e * a_ref[rows, :]

    zero = jnp.zeros((Q, e_ref.shape[1]), f32)
    first_ref[...] = lax.fori_loop(0, T, step, zero, unroll=8)


def back_gates_kernel(
    T,
    Q,
    e_ref,
    right_ref,
    zi_ref,
    zr_ref,
    conv_ref,
    state_ref,
    carry_ref,
    mask_ref,
    soft_ref,
    dzi_ref,
    dzr_ref,
    dconv_ref,
    ddecay_ref,
    tmpi_ref,
    tmpr_ref,
):
    soft = soft_ref[0:1, :]
    sig = soft_ref[1:2, :]

    def one(t, moved, total, prior):
        rows = pl.ds(pl.multiple_of(t * Q, Q), Q)
        keep = mask_ref[rows, :] >= 1.0
        e = e_ref[rows, :] + moved
        ig = jax.nn.sigmoid(zi_ref[rows, :])
        rg, a, rest = lru_parts(zr_ref[rows, :], soft)
        conv = conv_ref[rows, :]
        mult = jnp.where(keep, jnp.sqrt(rest), 1.0)
        dla = jnp.where(keep, e * a * prior - e * ig * conv * (a * a) / mult, 0.0)
        total = total + dla * rg
        tmpr_ref[rows, :] = dla * (-8.0 * soft) * rg * (1.0 - rg)
        em = e * mult
        tmpi_ref[rows, :] = em * conv * ig * (1.0 - ig)
        dconv_ref[rows, :] = em * ig
        return moved * jnp.where(keep, a, 0.0), total

    def step(i, carry):
        moved, total = carry
        t = T - 1 - i
        prior = state_ref[pl.ds(pl.multiple_of((t - 1) * Q, Q), Q), :]
        return one(t, moved, total, prior)

    zero = jnp.zeros((Q, e_ref.shape[1]), f32)
    moved, total = lax.fori_loop(0, T - 1, step, (right_ref[...], zero), unroll=4)
    _, total = one(0, moved, total, carry_ref[...])
    ddecay_ref[...] = 8.0 * sig * jnp.sum(total, axis=0, keepdims=True)

    def block(i, _):
        rows = pl.ds(pl.multiple_of(i * 64, 64), 64)
        dzi_ref[rows, :] = tmpi_ref[rows, :].astype(bf16)
        dzr_ref[rows, :] = tmpr_ref[rows, :].astype(bf16)
        return 0

    lax.fori_loop(0, T * Q // 64, block, 0)


def back_conv_kernel(
    T, Q, taps, dconv_ref, next_ref, pre_ref, halo_ref, mask_ref, w_ref, dus_ref, dw_ref, tmp_ref
):
    w = [w_ref[k : k + 1, :] for k in range(taps)]
    past = tuple(halo_ref[pl.ds((taps - 2 - k) * Q, Q), :] for k in range(taps - 1))
    zero = jnp.zeros((Q, pre_ref.shape[1]), f32)

    def terms(dconv, depth):
        return tuple(jnp.where(depth >= k, dconv, 0.0) for k in range(1, taps))

    def step(t, carry):
        past, waiting, sums = carry
        u = pre_ref[pl.ds(t, Q, stride=T), :].astype(bf16).astype(f32)
        rows = pl.ds(pl.multiple_of(t * Q, Q), Q)
        dconv = dconv_ref[rows, :]
        masked = terms(dconv, mask_ref[rows, :])
        done = waiting[taps - 2] + w[taps - 1] * masked[taps - 2]
        older = [w[0] * dconv]
        for k in range(1, taps - 1):
            older.append(waiting[k - 1] + w[k] * masked[k - 1])
        sums = (sums[0] + dconv * u,) + tuple(
            sums[k] + masked[k - 1] * past[k - 1] for k in range(1, taps)
        )

        @pl.when(t >= taps - 1)
        def _():
            tmp_ref[pl.ds(t - (taps - 1), Q, stride=T), :] = done

        return (u,) + past[:-1], tuple(older), sums

    start = (past, (zero,) * (taps - 1), (zero,) * taps)
    _, waiting, sums = lax.fori_loop(0, T, step, start, unroll=4)
    for j in range(taps - 1):
        rows = pl.ds(j * Q, Q)
        masked = terms(next_ref[rows, :], mask_ref[pl.ds((T + j) * Q, Q), :])
        done = waiting[taps - 2] + w[taps - 1] * masked[taps - 2]
        older = [zero]
        for k in range(1, taps - 1):
            older.append(waiting[k - 1] + w[k] * masked[k - 1])
        tmp_ref[pl.ds(T + j - (taps - 1), Q, stride=T), :] = done
        waiting = tuple(older)
    for k in range(taps):
        dw_ref[k : k + 1, :] = jnp.sum(sums[k], axis=0, keepdims=True)

    def block(i, _):
        rows = pl.ds(pl.multiple_of(i * 64, 64), 64)
        dus_ref[rows, :] = tmp_ref[rows, :].astype(bf16)
        return 0

    lax.fori_loop(0, T * Q // 64, block, 0)


def tiled_call(kernel, ins, outs, scratch=()):
    channels = outs[0][0][1]

    def spec(shape, first):
        return pl.BlockSpec((shape[0], LANES), (lambda c: (0, 0)) if first is None else (lambda c: (0, c + first)))

    moved = sum(a.size * a.dtype.itemsize for a, _ in ins)
    moved += sum(shape[0] * shape[1] * jnp.dtype(kind).itemsize for shape, kind in outs)
    work = outs[0][0][0] * channels
    return pl.pallas_call(
        kernel,
        grid=(pl.cdiv(channels, LANES),),
        in_specs=[spec(a.shape, first) for a, first in ins],
        out_specs=[spec(shape, 0) for shape, _ in outs],
        out_shape=[jax.ShapeDtypeStruct(shape, kind) for shape, kind in outs],
        scratch_shapes=[pltpu.VMEM((rows, LANES), f32) for rows in scratch],
        compiler_params=pltpu.CompilerParams(vmem_limit_bytes=VMEM_LIMIT),
        cost_estimate=pl.CostEstimate(flops=40 * work, bytes_accessed=moved, transcendentals=4 * work),
    )(*[a for a, _ in ins])


def assemble(places, blocks, rows_total, part, count, weights):
    columns = blocks[0].shape[1] // weights
    copies_total = ((len(blocks) - 1) * count + 1) * weights

    def kernel(places_ref, *refs):
        sources, outs, sems = refs[: len(blocks)], refs[len(blocks) : -1], refs[-1]
        copies = []

        def put(ref, start, rows, i):
            at = pl.multiple_of(places_ref[i], 16)
            for k, out in enumerate(outs):
                source = ref.at[pl.ds(start, rows), pl.ds(k * columns, columns)]
                copy = pltpu.make_async_copy(source, out.at[pl.ds(at, rows), :], sems.at[len(copies)])
                copy.start()
                copies.append(copy)

        i = 0
        for ref in sources[:-1]:
            for j in range(count):
                put(ref, j * part, part, i)
                i += 1
        put(sources[-1], 0, sources[-1].shape[0], i)
        for copy in copies:
            copy.wait()

    return pl.pallas_call(
        kernel,
        in_specs=[pl.BlockSpec(memory_space=pltpu.SMEM)] + [pl.BlockSpec(memory_space=pl.ANY)] * len(blocks),
        out_specs=[pl.BlockSpec(memory_space=pltpu.VMEM)] * weights,
        out_shape=[jax.ShapeDtypeStruct((rows_total, columns), blocks[0].dtype)] * weights,
        scratch_shapes=[pltpu.SemaphoreType.DMA((copies_total,))],
        compiler_params=pltpu.CompilerParams(vmem_limit_bytes=VMEM_LIMIT),
        cost_estimate=pl.CostEstimate(
            flops=0, bytes_accessed=4 * rows_total * columns * weights, transcendentals=0
        ),
    )(places, *blocks)


def norm_rows(values, count, rows, first_gain, order):
    width = values.shape[1]
    step = 16
    stride = values.shape[0] // count
    shard = width // count

    def kernel(order_ref, ref, out_ref, one_ref, two_ref):
        i = pl.program_id(0)

        @pl.when(i == 0)
        def _():
            for k in range(count):
                at = pl.ds(k * shard, shard)
                note = ref[pl.ds(k * stride + rows, step), pl.ds(0, shard)].astype(f32)
                one_ref[:, at] = jnp.broadcast_to(note[first_gain : first_gain + 1], (8, shard))
                two_ref[:, at] = jnp.broadcast_to(note[first_gain + 1 : first_gain + 2], (8, shard))

        def body(k, _):
            v = ref[pl.ds(pl.multiple_of(i * stride + k * step, step), step), :].astype(f32)
            scale = lax.rsqrt(jnp.mean(v * v, axis=-1, keepdims=True) + EPS)
            at = pl.ds(pl.multiple_of(k * step, step), step)
            out_ref[at, :] = (v * scale * one_ref[0:1, :]).astype(bf16)
            return 0

        lax.fori_loop(0, rows // step, body, 0, unroll=4)

    return pl.pallas_call(
        kernel,
        grid=(count,),
        in_specs=[pl.BlockSpec(memory_space=pltpu.SMEM), pl.BlockSpec(values.shape, lambda i: (0, 0))],
        out_specs=[
            pl.BlockSpec((rows, width), lambda i: (i, 0)),
            pl.BlockSpec((8, width), lambda i: (0, 0)),
            pl.BlockSpec((8, width), lambda i: (0, 0)),
        ],
        out_shape=[
            jax.ShapeDtypeStruct((rows * count, width), bf16),
            jax.ShapeDtypeStruct((8, width), f32),
            jax.ShapeDtypeStruct((8, width), f32),
        ],
        compiler_params=pltpu.CompilerParams(vmem_limit_bytes=VMEM_LIMIT),
        cost_estimate=pl.CostEstimate(
            flops=6 * rows * count * width, bytes_accessed=4 * rows * count * width, transcendentals=0
        ),
    )(order, values)


def after(value, *others):
    return lax.optimization_barrier((value,) + others)[0]


def per_device(
    seqs,
    wide,
    inputs,
    segments,
    cotangent,
    norm1_gain,
    gate_branch_w,
    linear_branch_w,
    conv_weight,
    input_gate_w,
    recur_gate_w,
    decay_param,
    out_proj_w,
    norm2_gain,
    mlp_gate_w,
    mlp_up_w,
    mlp_down_w,
):
    micro, _, T, D = inputs.shape
    length = segments.shape[2]
    Q = micro * wide
    chips = seqs // 2
    C = gate_branch_w.shape[1] // wide
    tiles = pl.cdiv(C, LANES)
    wide_C = tiles * LANES
    F = mlp_gate_w.shape[1] // wide
    block = input_gate_w.shape[1]
    taps = conv_weight.shape[1]
    own = micro * T
    shard = D // wide
    seq = lax.axis_index("seq")
    wsh = lax.axis_index("wsh")
    chip, core = seq // 2, seq % 2

    def perm_of(move_seq, flip=0):
        pairs = [(s, move_seq(s), w) for s in range(seqs) for w in range(wide)]
        return [(s * wide + w, d * wide + (w ^ flip)) for s, d, w in pairs if 0 <= d < seqs]

    def along_wsh(flip):
        return perm_of(lambda s: s, flip)

    def along_seq(shift):
        return perm_of(lambda s: s + shift)

    twin_perm = perm_of(lambda s: s ^ 1)
    pair_perm = perm_of(lambda s: s ^ 2)
    ring_perm = perm_of(lambda s: (s + 2) % seqs)
    assert chips == wide
    from_owner = [(k // wide * wide + k % wide, k % seqs * wide + k // seqs) for k in range(seqs * wide)]
    to_owner = [(b, a) for a, b in from_owner]

    def send(value, perm):
        return lax.ppermute(value, AXES, perm)

    def exchange(rows):
        return lax.all_to_all(rows, "wsh", split_axis=0, concat_axis=0, tiled=True)

    def gather(rows):
        return exchange(jnp.tile(rows, (wide, 1)))

    def added(rows):
        n = rows.shape[0] // wide
        return sum(rows[w * n : (w + 1) * n].astype(f32) for w in range(wide))

    def own_columns(weights, r, start, rows):
        parts = []
        for weight in weights:
            columns = weight.shape[1] // wide
            value = lax.dynamic_slice(weight, (start, (wsh ^ r) * columns), (rows, columns))
            parts.append(jnp.pad(value, ((0, 0), (0, -columns % LANES))))
        return jnp.concatenate(parts, axis=1)

    def fetch(weights, rows, at):
        got = [send(own_columns(weights, r, at * rows, rows), along_wsh(r)) for r in range(wide - 1, 0, -1)]
        return got[::-1]

    def place(weights, fetched, rows):
        places = [(wsh ^ r) * shard + at * rows for _, at in fetched for r in range(1, wide)]
        places = jnp.stack(places + [wsh * shard]).astype(jnp.int32)
        blocks = [value for value, _ in fetched] + [own_columns(weights, 0, 0, shard)]
        out = assemble(places, blocks, D, rows, wide - 1, len(weights))
        return [value[:, : w.shape[1] // wide] for value, w in zip(out, weights)]

    def strided(left, half):
        n = left.shape[1] // seqs
        return jnp.concatenate(
            [lax.dynamic_slice(left, (0, (2 * k + half) * n), (left.shape[0], n)) for k in range(chips)], axis=1
        )

    def halved(left, half):
        n = left.shape[1] // 2
        return lax.dynamic_slice(left, (0, half * n), (left.shape[0], n))

    def pair_terms(left, right, select):
        other = t_dot(select(left, 1 - core), right).astype(bf16)
        mine = t_dot(select(after(left, other), core), right).astype(bf16)
        return mine, send(other, twin_perm)

    def ring_chunk(pair, k):
        rows = pair[0].shape[0] // chips
        at = lax.rem(chip - k + chips, chips) * rows
        mine, other = [lax.dynamic_slice(p, (at, 0), (rows, p.shape[1])) for p in pair]
        return mine.astype(f32) + other.astype(f32)

    def pair_total(pair):
        return (pair[0].astype(f32) + pair[1].astype(f32)).astype(bf16)

    def swapped_chunk(swapped, k):
        rows = swapped.shape[0] // chips
        at = lax.rem(chip - k + chips, chips) * rows
        return lax.dynamic_slice(swapped, (at, 0), (rows, swapped.shape[1])).astype(f32)

    def ring_step(held, chunk):
        return send(held.astype(bf16), ring_perm).astype(f32) + chunk

    def columns_to_rows(value, weights, gain):
        rows, n = value.shape[0], value.shape[1] // 2
        weight_rows = [lax.dynamic_slice(w, (seq * rows, 0), (rows, w.shape[1])).astype(f32) for w in weights]
        own_gain = lax.dynamic_slice(gain, (seq * rows,), (rows,))
        term = jnp.sum(value[:, :n] * weight_rows[0], axis=1) + jnp.sum(value[:, n:] * weight_rows[1], axis=1)
        term = term / own_gain
        term_low = term.astype(bf16)
        rest = (term - term_low.astype(f32)).astype(bf16)
        extra = jnp.pad(jnp.stack([term_low, rest], axis=1), ((0, 0), (0, LANES - 2)))
        low = jnp.concatenate([value.astype(bf16), extra], axis=1)

        got = exchange(low).reshape(wide, rows // wide, low.shape[1])
        grads = [
            jnp.concatenate([got[w, :, k * n : (k + 1) * n].astype(f32) for w in range(wide)], axis=1) for k in range(2)
        ]
        total = jnp.sum(got[:, :, 2 * n : 2 * n + 2].astype(f32), axis=(0, 2))
        return grads[0], grads[1], total

    def dot(a, b):
        return jnp.dot(a, b, preferred_element_type=f32)

    def dot_t(a, b):
        return lax.dot_general(a, b, (((1,), (1,)), ((), ())), preferred_element_type=f32)

    def t_dot(a, b):
        return lax.dot_general(a, b, (((0,), (0,)), ((), ())), preferred_element_type=f32)

    def scale_of(v):
        return lax.rsqrt(jnp.mean(v * v, axis=-1, keepdims=True) + EPS)

    def norm_back(dn, v, gain):
        s = scale_of(v)
        scaled = dn * gain
        return s * scaled - v * (s * s * s) * jnp.mean(scaled * v, axis=-1, keepdims=True)

    def neighbours(weights, held):
        here, there = seq % 4, seq % 4 ^ 2
        paired = send(held, pair_perm)

        def parts():
            return [
                (held, here),
                (paired, there),
                (send(held, twin_perm), here ^ 1),
                (send(paired, twin_perm), there ^ 1),
            ]

        return paired, lambda: place(weights, parts(), shard // 4)

    branch = [gate_branch_w, linear_branch_w]
    held = fetch(branch, shard // 4, seq % 4)

    small = jnp.concatenate([input_gate_w, recur_gate_w, conv_weight, decay_param[:, None]], axis=1)
    pad = -small.shape[1] % LANES
    small = send(jnp.pad(small, ((0, 0), (0, pad))), from_owner)
    held, small = lax.optimization_barrier((held, small))
    held = jnp.concatenate(held, axis=0)
    _, place_branch = neighbours(branch, held)
    w_gate, w_linear = place_branch()
    small_rows = small.shape[0]
    small = small[None]
    for b in range(seqs.bit_length() - 1):
        small = jnp.concatenate([small, send(small, perm_of(lambda s: s ^ (1 << b)))], axis=0)
    joined = jnp.zeros((C, small.shape[2]), bf16)
    for k in range(seqs):
        joined = lax.dynamic_update_slice(joined, small[k], ((seq ^ k) * small_rows, 0))
    small = joined

    rows = jnp.pad(segments[:, 0], ((0, 0), (taps - 1, taps - 1)), constant_values=-1)
    whole_depth = jnp.zeros((micro, length + taps - 1), f32)
    for k in range(1, taps):
        same = rows[:, taps - 1 :] == rows[:, taps - 1 - k : rows.shape[1] - k]
        same = same & (jnp.arange(length + taps - 1) >= k)[None, :]
        whole_depth = whole_depth + same.astype(f32)
    depth = lax.dynamic_slice(whole_depth, (0, seq * T), (micro, T + taps - 1)).astype(bf16)

    note = jnp.zeros((16, D), bf16)
    note = note.at[:micro, : T + taps - 1].set(depth)
    note = note.at[micro, :shard].set(norm1_gain)
    note = note.at[micro + 1, :shard].set(norm2_gain)
    noted = jnp.concatenate([inputs[:, 0].reshape(own, D), note], axis=0)
    x_group = gather(after(noted, held))
    depth = x_group.reshape(wide, own + 16, D)[:, own : own + micro, : T + taps - 1]
    depth = depth.reshape(Q, T + taps - 1).astype(f32)
    mask = jnp.broadcast_to(depth.T[:, :, None], (T + taps - 1, Q, LANES)).reshape(-1, LANES)
    mask_own = mask[: T * Q]

    in_gate = small[:, :block]
    rec_gate = small[:, block : 2 * block]
    conv_w = small[:, 2 * block : 2 * block + taps].astype(f32).T
    conv_w = jnp.pad(conv_w, ((0, 8 - taps), (0, 0)))
    decay = small[:, 2 * block + taps].astype(f32)
    soft = jnp.stack([jax.nn.softplus(-decay), jax.nn.sigmoid(-decay)])
    soft = jnp.pad(soft, ((0, 6), (0, 0)))
    blocks = C // block

    def dense(gate_w):
        slabs = []
        for b in range(blocks):
            slab = gate_w[b * block : (b + 1) * block]
            slabs.append(jnp.pad(slab, ((0, 0), (b * block, wide_C - (b + 1) * block))))
        return jnp.concatenate(slabs, axis=0)

    gates_w = jnp.concatenate([dense(in_gate), dense(rec_gate)], axis=1)

    order = after(jnp.zeros((1,), jnp.int32), w_gate, gates_w)
    xn, gain_one, gain_two = norm_rows(x_group, wide, own, micro, order)
    gain_one, gain_two = gain_one[0], gain_two[0]
    last = xn.reshape(Q, T, D)[:, T - (taps - 1) :].transpose(1, 0, 2).reshape((taps - 1) * Q, D)
    halo = send(dot(last, w_linear).astype(bf16), along_seq(1)).astype(f32)
    us_pre = dot(xn, w_linear)

    mlp = [mlp_gate_w, mlp_up_w]
    mlp_held = fetch([after(w, xn) for w in mlp], shard // 4, seq % 4)
    g_group = gather(after(cotangent[:, 0].reshape(own, D), x_group))

    (conv,) = tiled_call(
        partial(conv_kernel, T, Q, taps),
        [(us_pre, 0), (halo, 0), (mask_own, None), (conv_w, 0)],
        [((T * Q, C), f32)],
    )
    conv_low = conv.astype(bf16)
    z = dot(conv_low, gates_w)
    h_local, a, end = tiled_call(
        partial(scan_kernel, T, Q),
        [(z, 0), (z, tiles), (conv, 0), (mask_own, None), (soft, 0)],
        [((T * Q, C), f32), ((T * Q, C), f32), ((2 * Q, C), f32)],
    )
    reach = pl.cdiv(length // 4, T)
    ends = [send(end, along_seq(k)) for k in range(1, reach + 1)]
    following_ends = [send(end[Q:], along_seq(-k)) for k in range(1, reach)]
    ends, following_ends = lax.optimization_barrier((ends, following_ends))
    ypre = dot(after(xn, end), w_gate)
    carry, through = ends[0][:Q], ends[0][Q:]
    for value in ends[1:]:
        carry = carry + through * value[:Q]
        through = through * value[Q:]
    state, hs, prod = tiled_call(
        partial(carry_kernel, T, Q),
        [(h_local, 0), (a, 0), (carry, 0), (ypre, 0)],
        [((T * Q, C), f32), ((T * Q, C), bf16), ((T * Q, C), bf16)],
        [T * Q],
    )
    x_own = inputs[:, 0].reshape(own, D).astype(f32)
    product, mlp_held, g_group = lax.optimization_barrier((dot(prod, out_proj_w).astype(bf16), mlp_held, g_group))
    mlp_held = jnp.concatenate(mlp_held, axis=0)
    mlp_paired, place_mlp = neighbours(mlp, mlp_held)
    got, _ = lax.optimization_barrier((exchange(product), mlp_paired))
    hidden = x_own + added(got)
    hn_own = (hidden * scale_of(hidden) * gain_two).astype(bf16)
    w_gate2, w_up = place_mlp()
    hn, w_gate2, w_up = lax.optimization_barrier((gather(hn_own), w_gate2, w_up))
    gpre = dot(hn, w_gate2).astype(bf16)
    uppre = dot(hn, w_up).astype(bf16)
    gpre, uppre = lax.optimization_barrier((gpre, uppre))
    act = (gelu_parts(gpre.astype(f32))[0] * uppre.astype(f32)).astype(bf16)

    g_own = cotangent[:, 0].reshape(own, D).astype(f32)
    down_pair = pair_terms(act, g_group, halved)
    dact = dot_t(after(g_group, down_pair[0]), mlp_down_w)
    act_gate, act_slope = gelu_parts(gpre.astype(f32))
    dgp = (dact * uppre.astype(f32) * act_slope).astype(bf16)
    dup = (dact * act_gate).astype(bf16)
    total, dgp, dup = lax.optimization_barrier((pair_total(down_pair), dgp, dup))
    down = exchange(total)
    product = (dot_t(dgp, w_gate2) + dot_t(dup, w_up)).astype(bf16)

    def down_step(k, held):
        return ring_step(held, swapped_chunk(down, k)) if k <= chips else held

    down_sum = swapped_chunk(down, 1).astype(bf16)
    product, down_sum, hn, dgp, dup = lax.optimization_barrier((product, down_sum, hn, dgp, dup))
    mlp_terms = t_dot(hn, jnp.concatenate([dgp, dup], axis=1)).astype(bf16)
    got, down_sum, mlp_terms = lax.optimization_barrier((exchange(product), down_step(2, down_sum), mlp_terms))
    mlp_sum = lax.psum_scatter(mlp_terms, "seq", scatter_dimension=0, tiled=True).astype(f32)
    dh1 = g_own + norm_back(added(got), hidden, gain_two)

    do_own, act_late = lax.optimization_barrier((dh1.astype(bf16), act))
    product = dot(act_late, mlp_down_w).astype(bf16)
    do, down_sum, product = lax.optimization_barrier((gather(do_own), down_step(3, down_sum), product))
    got = exchange(product)
    for k in range(4, chips + 1):
        down_sum = down_step(k, down_sum)
    dprod = dot_t(do, out_proj_w)
    dy, e_local, first = tiled_call(
        partial(back_scan_kernel, T, Q),
        [(dprod, 0), (ypre, 0), (hs, 0), (a, 0)],
        [((T * Q, C), bf16), ((T * Q, C), f32), ((Q, C), f32)],
        [T * Q],
    )
    firsts = [send(first, along_seq(-k)) for k in range(1, reach + 1)]
    out_terms = t_dot(after(prod, first), do).astype(bf16)
    right, through = firsts[0], None
    for value, past in zip(firsts[1:], following_ends):
        through = past if through is None else through * past
        right = right + through * value
    dzi, dzr, dconv_direct, ddecay = tiled_call(
        partial(back_gates_kernel, T, Q),
        [
            (e_local, 0),
            (right, 0),
            (z, 0),
            (z, tiles),
            (conv, 0),
            (state, 0),
            (carry, 0),
            (mask_own, None),
            (soft, 0),
        ],
        [((T * Q, C), bf16), ((T * Q, C), bf16), ((T * Q, C), f32), ((1, C), f32)],
        [T * Q, T * Q],
    )
    dconv = dconv_direct + dot_t(dzi, gates_w[:, :C]) + dot_t(dzr, gates_w[:, wide_C : wide_C + C])
    following = send(dconv[: (taps - 1) * Q].astype(bf16), along_seq(-1)).astype(f32)
    following, got, down_sum = lax.optimization_barrier((following, got, down_sum))
    dus, dconv_w = tiled_call(
        partial(back_conv_kernel, T, Q, taps),
        [(dconv, 0), (following, 0), (us_pre, 0), (halo, 0), (mask, None), (conv_w, 0)],
        [((T * Q, C), bf16), ((8, C), f32)],
        [T * Q],
    )

    block_output = hidden + added(got)
    branch_pair = pair_terms(xn, jnp.concatenate([dy, dus], axis=1), strided)
    branch_sum = ring_chunk(branch_pair, 1).astype(bf16)

    def diagonal(terms):
        return jnp.concatenate(
            [terms[b * block : (b + 1) * block, b * block : (b + 1) * block] for b in range(blocks)], axis=0
        )

    small_terms = jnp.concatenate(
        [
            diagonal(t_dot(conv_low, dzi)),
            diagonal(t_dot(conv_low, dzr)),
            dconv_w[:taps].T,
            ddecay.T,
            jnp.zeros((C, pad), f32),
        ],
        axis=1,
    )

    def branch_step(k, held):
        return ring_step(held, ring_chunk(branch_pair, k)) if k <= chips else held

    dy_late, dus_late, branch_sum, small_terms = lax.optimization_barrier((dy, dus, branch_sum, small_terms))
    row_terms = jnp.concatenate([out_terms, small_terms.astype(bf16)], axis=1)
    row_sum = lax.psum_scatter(row_terms, "seq", scatter_dimension=0, tiled=True)
    product = (dot_t(dy_late, w_gate) + dot_t(dus_late, w_linear)).astype(bf16)
    product, branch_sum = lax.optimization_barrier((product, branch_step(2, branch_sum)))
    got = exchange(product)
    for k in range(3, chips + 1):
        branch_sum = branch_step(k, branch_sum)
    got, branch_sum = lax.optimization_barrier((got, branch_sum))
    dxn = added(got)
    row_sum = send(after(row_sum, got), to_owner).astype(f32)
    out_sum, small_sum = row_sum[:, :D], row_sum[:, D:]
    input_grad = dh1 + norm_back(dxn, x_own, gain_one)
    gate2_grad, up_grad, gain_two_grad = columns_to_rows(after(mlp_sum, got), [w_gate2, w_up], gain_two)
    gate_grad, linear_grad, gain_one_grad = columns_to_rows(branch_sum, [w_gate, w_linear], gain_one)
    return (
        block_output.reshape(inputs.shape),
        input_grad.reshape(inputs.shape),
        gain_one_grad,
        gate_grad,
        linear_grad,
        small_sum[:, 2 * block : 2 * block + taps],
        small_sum[:, :block],
        small_sum[:, block : 2 * block],
        small_sum[:, 2 * block + taps],
        out_sum,
        gain_two_grad,
        gate2_grad,
        up_grad,
        down_sum,
    )


def solution(mesh):
    both = ("seq", "wsh")
    tokens = P(None, "wsh", "seq", None)
    return jax.shard_map(
        partial(per_device, mesh.shape["seq"], mesh.shape["wsh"]),
        mesh=mesh,
        in_specs=(
            tokens,
            P(None, "wsh", None),
            tokens,
            P("wsh"),
            P("wsh", None),
            P("wsh", None),
            P(both, None),
            P(both, None),
            P(both, None),
            P(both),
            P("wsh", None),
            P("wsh"),
            P("wsh", None),
            P("wsh", None),
            P("wsh", None),
        ),
        out_specs=(
            tokens,
            tokens,
            P(both),
            P(both, None),
            P(both, None),
            P(both, None),
            P(both, None),
            P(both, None),
            P(both),
            P(both, None),
            P(both),
            P(both, None),
            P(both, None),
            P(both, None),
        ),
        check_vma=False,
    )
```
